128 devices in a mesh: dp: 4 (over x_hi, core), feat: 32 (over y, z, x_lo).
Axes of the slice: x: 4 (x_hi: 2, x_lo: 2; x = x_hi * 2 + x_lo), y: 4, z: 4, core: 2. Of those that a mesh axis runs over, the one named last changes fastest.
Arguments:
- tokens: bfloat16 [4096, 16384], P('dp', 'feat'), may hold values from -6 to 6
- butterfly: bfloat16 [16384, 3072], P('feat'), may hold values from -0.109375 to 0.109375
- left_factor: bfloat16 [16384, 256], P('feat'), may hold values from -0.046875 to 0.046875
- right_factor: bfloat16 [256, 16384], P(None, 'feat'), may hold values from -0.375 to 0.375
- cotangent: bfloat16 [4096, 16384], P('dp', 'feat'), may hold values from -6 to 6
Outputs:
- output: bfloat16 [4096, 16384], P('dp', 'feat')
- grad_tokens: bfloat16 [4096, 16384], P('dp', 'feat')
- grad_butterfly: float32 [16384, 3072], P('feat')
- grad_left: float32 [16384, 256], P('feat')
- grad_right: float32 [256, 16384], P(None, 'feat')
The draws below stay inside these ranges and needn't reach their ends.
All inputs are finite; a program needn't handle non-finite values.
Results may differ from the reference program's by a relative error of at most 0.0057.
Values may be sent and summed in bfloat16 or wider, within the bound.
No kernel may reach another device: no remote copies, remote signals or barrier semaphores. Data moves between devices by JAX's collectives and lax.ppermute only.
A program may use at most 128 MiB of HBM per device.

```python
import jax
import jax.numpy as jnp
import numpy as np
from jax import lax

BS = 512
RANK = 256
LOG = 5
WIDTH = 16384
TOKENS = 4096
N_FEAT = 32


def block_levels(stream_key, extent, pieces, low, high):
    def one(dim, blocks):
        steps = jax.random.uniform(jax.random.fold_in(jax.random.fold_in(stream_key, 6), dim), (blocks,), jnp.float32, low / len(pieces), high / len(pieces))
        return jnp.repeat(jnp.exp(steps), extent[dim] // blocks).reshape((-1,) + (1,) * (len(extent) - dim - 1))

    level = one(*pieces[0])
    for cut in pieces[1:]:
        level = level * one(*cut)
    return level


def centred(stream_key, extent, scale, limit, shards=(), kind=jnp.bfloat16):
    factor_of = block_levels(stream_key, extent, shards, -0.22, 0.18) if shards else 1.0
    array = jax.random.normal(stream_key, extent, jnp.float32) * scale * factor_of
    return jnp.minimum(jnp.maximum(array, -limit), limit).astype(kind)


def setup_inputs(seed: int = 0) -> dict:
    key_list = jax.random.split(jax.random.key(seed), 6)
    return {
        "tokens": centred(key_list[0], (TOKENS, WIDTH), 1.0, 6.0, ((0, 4), (1, 32))),
        "butterfly": centred(key_list[1], (WIDTH, (LOG + 1) * BS), (BS * (LOG + 1)) ** -0.5, 0.109375, ((0, 32),)),
        "left_factor": centred(key_list[2], (WIDTH, RANK), WIDTH ** -0.5, 0.046875, ((0, 32),)),
        "right_factor": centred(key_list[3], (RANK, WIDTH), RANK ** -0.5, 0.375, ((1, 32),)),
        "cotangent": centred(key_list[4], (TOKENS, WIDTH), 1.0, 6.0, ((0, 4), (1, 32))),
    }


def partner_table(blocks, count):
    table = np.zeros((count, blocks), dtype=np.int32)
    for slot in range(count):
        for index in range(blocks):
            table[slot, index] = index if slot == 0 else index ^ (1 << (slot - 1))
    return table


def normal_cdf(value):
    return 0.5 * (1.0 + lax.erf(value * 0.7071067811865476))


def reference(tokens, butterfly, left_factor, right_factor, cotangent):
    blocks = N_FEAT
    count = LOG + 1
    table = partner_table(blocks, count)
    rows = tokens.shape[0]
    tok_blocks = tokens.astype(jnp.float32).reshape(rows, blocks, BS)
    weights = butterfly.astype(jnp.float32).reshape(blocks, BS, count, BS)
    reduced = jnp.dot(tokens, left_factor, preferred_element_type=jnp.float32).astype(jnp.bfloat16)
    pre = jnp.dot(reduced, right_factor, preferred_element_type=jnp.float32).reshape(rows, blocks, BS)
    for slot in range(count):
        moved = tok_blocks[:, table[slot], :]
        pre = pre + jnp.einsum('tir,irc->tic', moved, weights[:, :, slot, :])
    output = (pre * normal_cdf(pre)).astype(jnp.bfloat16).reshape(rows, blocks * BS)
    density = jnp.exp(-0.5 * pre * pre) * 0.3989422804014327
    delta = (cotangent.astype(jnp.float32).reshape(rows, blocks, BS) * (normal_cdf(pre) + pre * density)).astype(jnp.bfloat16)
    delta_f = delta.astype(jnp.float32)
    grads = []
    back = jnp.zeros((rows, blocks, BS), jnp.float32)
    for slot in range(count):
        moved = tok_blocks[:, table[slot], :]
        grads.append(jnp.einsum('tir,tic->irc', moved, delta_f))
        term = jnp.einsum('tic,irc->tir', delta_f, weights[:, :, slot, :])
        back = back + term[:, table[slot], :]
    grad_butterfly = jnp.stack(grads, axis=2).reshape(blocks * BS, count * BS)
    delta_flat = delta.reshape(rows, blocks * BS)
    grad_right = jnp.dot(reduced.T, delta_flat, preferred_element_type=jnp.float32)
    back_reduced = jnp.dot(delta_flat, right_factor.T, preferred_element_type=jnp.float32).astype(jnp.bfloat16)
    grad_left = jnp.dot(tokens.T, back_reduced, preferred_element_type=jnp.float32)
    back = back.reshape(rows, blocks * BS) + jnp.dot(back_reduced, left_factor.T, preferred_element_type=jnp.float32)
    return output, back.astype(jnp.bfloat16), grad_butterfly, grad_left, grad_right
```

```python
import jax
import jax.numpy as jnp
from jax import lax
from jax.sharding import PartitionSpec as P

BF = jnp.bfloat16
F32 = jnp.float32


def flip(block, axis, mask):
    count = lax.axis_size(axis)
    return lax.ppermute(block, axis, [(i, i ^ mask) for i in range(count)])


def normal_cdf(value):
    return 0.5 * (1.0 + lax.erf(value * 0.7071067811865476))


def contract(first, second, first_dim, second_dim):
    return lax.dot_general(
        first, second, (((first_dim,), (second_dim,)), ((), ())), preferred_element_type=F32
    )


def sum_over_feat(part):
    count = lax.axis_size("feat")
    rows, width = part.shape
    pieces = part.astype(BF).reshape(count, rows // count, width)
    pieces = lax.all_to_all(pieces, "feat", 0, 0)
    mine = jnp.sum(pieces.astype(F32), axis=0).astype(BF)
    copies = jnp.broadcast_to(mine[None], (count, rows // count, width))
    return lax.all_to_all(copies, "feat", 0, 0).reshape(rows, width)


def shards(tokens, butterfly, left_factor, right_factor, cotangent):
    bs = tokens.shape[1]
    rows = tokens.shape[0]
    half = rows // 2
    core = lax.axis_index("dp") & 1

    def weight_block(slot):
        return butterfly[:, slot * bs : (slot + 1) * bs]

    first, second = tokens[:half], tokens[half:]
    t0 = flip(tokens, "feat", 1)
    t1a, t3a = flip(first, "feat", 2), flip(first, "feat", 8)
    t1b, t3b = flip(second, "feat", 2), flip(second, "feat", 8)
    t2b, t4b = flip(second, "feat", 4), flip(second, "feat", 16)
    reduced = sum_over_feat(jnp.dot(tokens, left_factor, preferred_element_type=F32))
    t2a, t4a = flip(t1a, "feat", 6), flip(t3a, "feat", 24)

    def both(a, b):
        return jnp.concatenate([a, b], axis=0)

    blocks = [tokens, t0, both(t1a, t1b), both(t2a, t2b), both(t3a, t3b), both(t4a, t4b)]
    pre = jnp.dot(reduced, right_factor, preferred_element_type=F32)
    for slot, block in enumerate(blocks):
        pre = pre + jnp.dot(block, weight_block(slot), preferred_element_type=F32)
    cdf = normal_cdf(pre)
    output = (pre * cdf).astype(BF)
    density = jnp.exp(-0.5 * pre * pre) * 0.3989422804014327
    delta = (cotangent.astype(F32) * (cdf + pre * density)).astype(BF)

    back = contract(delta, weight_block(0), 1, 1)
    sent = []
    for level in (0, 2, 4, 1, 3):
        part = contract(delta, weight_block(level + 1), 1, 1).astype(BF)
        sent.append(flip(part, "feat", 1 << level))

    hc = bs // 2
    keep = lax.dynamic_slice_in_dim(delta, core * hc, hc, 1)
    give = lax.dynamic_slice_in_dim(delta, (1 - core) * hc, hc, 1)

    def over_dp(lefts, give, keep):
        got = flip(jnp.concatenate([contract(l, give, 0, 0) for l in lefts], 0).astype(BF), "dp", 1)
        mine = jnp.concatenate([contract(l, keep, 0, 0) for l in lefts], 0)
        mine = (mine + got.astype(F32)).astype(BF)
        total = mine.astype(F32) + flip(mine, "dp", 2).astype(F32)
        other = flip(total, "dp", 1)
        return jnp.where(core == 0, total, other), jnp.where(core == 0, other, total)

    lo1, hi1 = over_dp(blocks[:3], give, keep)
    lo2, hi2 = over_dp(blocks[3:] + [reduced], give, keep)

    back_reduced = sum_over_feat(contract(delta, right_factor, 1, 1))
    hr = back_reduced.shape[1] // 2
    keep_l = lax.dynamic_slice_in_dim(back_reduced, core * hr, hr, 1)
    give_l = lax.dynamic_slice_in_dim(back_reduced, (1 - core) * hr, hr, 1)
    lo3, hi3 = over_dp([tokens], give_l, keep_l)
    grad_left = jnp.concatenate([lo3, hi3], 1)
    grad_right = jnp.concatenate([lo2[3 * bs :], hi2[3 * bs :]], 1)
    parts = []
    for lo, hi in ((lo1, hi1), (lo2, hi2)):
        for k in range(3):
            parts += [lo[k * bs : (k + 1) * bs], hi[k * bs : (k + 1) * bs]]
    grad_butterfly = jnp.concatenate(parts, 1)

    back = back + contract(back_reduced, left_factor, 1, 1)
    for part in sent:
        back = back + part.astype(F32)
    return (output, back.astype(BF), grad_butterfly, grad_left, grad_right)


def solution(mesh):
    in_specs = (P("dp", "feat"), P("feat", None), P("feat", None), P(None, "feat"), P("dp", "feat"))
    out_specs = (
        P("dp", "feat"),
        P("dp", "feat"),
        P("feat", None),
        P("feat", None),
        P(None, "feat"),
    )
    return jax.shard_map(shards, mesh=mesh, in_specs=in_specs, out_specs=out_specs, check_vma=False)
```

```python
import functools

import jax
import jax.numpy as jnp
from jax import lax
from jax.experimental import pallas as pl
from jax.experimental.pallas import tpu as pltpu
from jax.sharding import PartitionSpec as P

BF = jnp.bfloat16
F32 = jnp.float32
TILE = 256


def flip(block, axis, mask):
    count = lax.axis_size(axis)
    return lax.ppermute(block, axis, [(i, i ^ mask) for i in range(count)])


def normal_cdf(value):
    return 0.5 * (1.0 + lax.erf(value * 0.7071067811865476))


def contract(first, second, first_dim, second_dim):
    return lax.dot_general(
        first, second, (((first_dim,), (second_dim,)), ((), ())), preferred_element_type=F32
    )


def struct(*shape_and_type):
    *shape, kind = shape_and_type
    return jax.ShapeDtypeStruct(tuple(shape), kind)


def call(kernel, outs, *args, name, vmem=40, **more):
    return pl.pallas_call(
        kernel,
        out_shape=outs,
        name=name,
        compiler_params=pltpu.CompilerParams(vmem_limit_bytes=vmem << 20),
        cost_estimate=pl.CostEstimate(flops=1000, bytes_accessed=1000, transcendentals=0),
        **more,
    )(*args)


def low_kernel(x, w, o):
    o[...] = jnp.dot(x[...], w[...], preferred_element_type=F32).astype(BF)


def sum_kernel(pieces, copies):
    count = pieces.shape[0]
    total = pieces[0].astype(F32)
    for k in range(1, count):
        total = total + pieces[k].astype(F32)
    mine = total.astype(BF)
    for k in range(count):
        copies[k] = mine


def forward_kernel(slots, reduced, right, cotangent, weight, *refs):
    blocks, (output, delta) = refs[:-2], refs[-2:]
    rows, bs = output.shape
    for row in range(0, rows, TILE):
        here = slice(row, row + TILE)
        pre = jnp.dot(reduced[here, :], right[...], preferred_element_type=F32)
        for slot, parts in enumerate(slots):
            size = rows // len(parts)
            ref = blocks[parts[row // size]]
            inside = slice(row % size, row % size + TILE)
            pre = pre + jnp.dot(
                ref[inside, :], weight[:, slot * bs : (slot + 1) * bs], preferred_element_type=F32
            )
        cdf = normal_cdf(pre)
        output[here, :] = (pre * cdf).astype(BF)
        density = jnp.exp(-0.5 * pre * pre) * 0.3989422804014327
        delta[here, :] = (cotangent[here, :].astype(F32) * (cdf + pre * density)).astype(BF)


def half_dots(slots, blocks, cols, hc):
    out = []
    for parts in slots:
        total = None
        row = 0
        for k in parts:
            term = contract(blocks[k][...], cols[row : row + blocks[k].shape[0], :], 0, 0)
            total = term if total is None else total + term
            row += blocks[k].shape[0]
        out.append(total)
    return out


def give_kernel(slots, core, delta, *refs):
    blocks, out = refs[:-1], refs[-1]
    hc = delta.shape[1] // 2

    def run(cols):
        row = 0
        for total in half_dots(slots, blocks, cols, hc):
            out[row : row + total.shape[0], :] = total.astype(out.dtype)
            row += total.shape[0]

    @pl.when(core[0] == 0)
    def _():
        run(delta[:, hc:])

    @pl.when(core[0] == 1)
    def _():
        run(delta[:, :hc])


def keep_kernel(slots, core, delta, got, *refs):
    blocks, out = refs[:-1], refs[-1]
    hc = delta.shape[1] // 2

    def run(cols):
        row = 0
        for total in half_dots(slots, blocks, cols, hc):
            here = slice(row, row + total.shape[0])
            out[here, :] = (total + got[here, :].astype(F32)).astype(out.dtype)
            row += total.shape[0]

    @pl.when(core[0] == 0)
    def _():
        run(delta[:, :hc])

    @pl.when(core[0] == 1)
    def _():
        run(delta[:, hc:])


def back_kernel(slots, delta, weight, *outs):
    bs = delta.shape[1]
    for slot, out in zip(slots, outs):
        out[...] = contract(delta[...], weight[:, slot * bs : (slot + 1) * bs], 1, 1).astype(
            out.dtype
        )


def local_back_kernel(delta, right, out):
    out[...] = contract(delta[...], right[...], 1, 1).astype(BF)


def finish_kernel(delta, weight, back_reduced, left, *refs):
    parts, out = refs[:-1], refs[-1]
    rows, bs = out.shape
    for row in range(0, rows, TILE):
        here = slice(row, row + TILE)
        total = contract(delta[here, :], weight[:, :bs], 1, 1)
        total = total + contract(back_reduced[here, :], left[...], 1, 1)
        for part in parts:
            total = total + part[here, :].astype(F32)
        out[here, :] = total.astype(BF)


def assemble_kernel(count, with_old, core, *refs):
    mine, recv, mine_o, recv_o = refs[:4]
    outs = refs[4 + with_old :]

    def run(a, b, c, d):
        hc = a.shape[1]
        out = outs[0]
        out[:, :hc] = a[...].astype(F32) + b[...].astype(F32)
        out[:, hc:] = c[...].astype(F32) + d[...].astype(F32)

    @pl.when(core[0] == 0)
    def _():
        run(mine, recv, mine_o, recv_o)

    @pl.when(core[0] == 1)
    def _():
        run(mine_o, recv_o, mine, recv)


def assemble(core, four, out, steps, in_start, out_start, old, name):
    hc = four[0].shape[1]
    bs = out.shape[0]
    half = pl.BlockSpec((bs, hc), lambda k: (k + in_start, 0))
    more = {}
    specs = [pl.BlockSpec(memory_space=pltpu.SMEM)] + [half] * 4
    args = [core, *four]
    if old is not None:
        specs.append(pl.BlockSpec(memory_space=pl.ANY))
        args.append(old)
        more["input_output_aliases"] = {5: 0}
    return call(
        functools.partial(assemble_kernel, steps, old is not None),
        out,
        *args,
        name=name,
        grid=(steps,),
        in_specs=specs,
        out_specs=pl.BlockSpec((bs, 2 * hc), lambda k: (0, k + out_start)),
        **more,
    )


def sum_over_feat(part, name):
    count = lax.axis_size("feat")
    rows, width = part.shape
    shape = (count, rows // count, width)
    pieces = lax.all_to_all(part.reshape(shape), "feat", 0, 0)
    copies = call(sum_kernel, struct(*shape, BF), pieces, name=name)
    return lax.all_to_all(copies, "feat", 0, 0).reshape(rows, width)


def shards(tokens, butterfly, left_factor, right_factor, cotangent):
    rows, bs = tokens.shape
    rank = left_factor.shape[1]
    half = rows // 2
    hc = bs // 2
    core = (lax.axis_index("dp") & 1).astype(jnp.int32).reshape(1)
    smem = pl.BlockSpec(memory_space=pltpu.SMEM)
    whole = pl.BlockSpec()

    first, second = tokens[:half], tokens[half:]
    t0 = flip(tokens, "feat", 1)
    t1a, t3a = flip(first, "feat", 2), flip(first, "feat", 8)
    t1b, t3b = flip(second, "feat", 2), flip(second, "feat", 8)
    t2b, t4b = flip(second, "feat", 4), flip(second, "feat", 16)
    low = call(low_kernel, struct(rows, rank, BF), tokens, left_factor, name="low")
    reduced = sum_over_feat(low, "low_sum")
    t2a, t4a = flip(t1a, "feat", 6), flip(t3a, "feat", 24)

    blocks = (tokens, t0, t1a, t1b, t2a, t2b, t3a, t3b, t4a, t4b)
    slots = ((0,), (1,), (2, 3), (4, 5), (6, 7), (8, 9))
    output, delta = call(
        functools.partial(forward_kernel, slots),
        (struct(rows, bs, BF), struct(rows, bs, BF)),
        reduced,
        right_factor,
        cotangent,
        butterfly,
        *blocks,
        name="forward",
    )

    (c0,) = call(functools.partial(back_kernel, (1,)), (struct(rows, bs, BF),), delta, butterfly, name="back_x")
    r0 = flip(c0, "feat", 1)
    local_back = call(local_back_kernel, struct(rows, rank, BF), delta, right_factor, name="local_back")

    def specs(n):
        return [smem] + [whole] * n

    chunks = (
        ((0,), (1,), (2, 3)),
        ((4, 5), (6, 7), (8, 9), (10,)),
    )
    every = blocks + (reduced,)

    def renumber(chunk):
        used = [k for parts in chunk for k in parts]
        return [every[k] for k in used], tuple(tuple(used.index(k) for k in parts) for parts in chunk)

    gots = []
    for index, chunk in enumerate(chunks):
        used, local = renumber(chunk)
        height = sum(every[parts[0]].shape[1] for parts in chunk)
        give = call(
            functools.partial(give_kernel, local),
            struct(height, hc, BF),
            core,
            delta,
            *used,
            name=f"give{index}",
            in_specs=specs(1 + len(used)),
        )
        gots.append(flip(give, "dp", 1))
    c2, c4, c1, c3 = call(
        functools.partial(back_kernel, (3, 5, 2, 4)),
        (struct(rows, bs, BF),) * 4,
        delta,
        butterfly,
        name="back_yz",
    )
    r2, r4 = flip(c2, "feat", 4), flip(c4, "feat", 16)
    r1, r3 = flip(c1, "feat", 2), flip(c3, "feat", 8)
    fours = []
    for index, chunk in enumerate(chunks):
        used, local = renumber(chunk)
        mine = call(
            functools.partial(keep_kernel, local),
            struct(*gots[index].shape, BF),
            core,
            delta,
            gots[index],
            *used,
            name=f"keep{index}",
            in_specs=specs(2 + len(used)),
        )
        recv = flip(mine, "dp", 2)
        fours.append((mine, recv, flip(mine, "dp", 1), flip(recv, "dp", 1)))

    back_reduced = sum_over_feat(local_back, "back_sum")
    give = call(
        functools.partial(give_kernel, ((0,),)),
        struct(bs, rank // 2, BF),
        core,
        back_reduced,
        tokens,
        name="give_left",
        in_specs=specs(2),
    )
    got = flip(give, "dp", 1)
    mine = call(
        functools.partial(keep_kernel, ((0,),)),
        struct(bs, rank // 2, BF),
        core,
        back_reduced,
        got,
        tokens,
        name="keep_left",
        in_specs=specs(3),
    )
    recv = flip(mine, "dp", 2)
    left_four = (mine, recv, flip(mine, "dp", 1), flip(recv, "dp", 1))

    grads = struct(*butterfly.shape, F32)
    grads_a = assemble(core, fours[0], grads, 3, 0, 0, None, "put0")
    grad_butterfly = assemble(core, fours[1], grads, 3, 0, 3, grads_a, "put1")
    grad_right = assemble(
        core, fours[1], struct(rank, bs, F32), 1, 3 * bs // rank, 0, None, "put_right"
    )
    grad_left = assemble(core, left_four, struct(bs, rank, F32), 1, 0, 0, None, "put_left")

    grad_tokens = call(
        finish_kernel,
        struct(rows, bs, BF),
        delta,
        butterfly,
        back_reduced,
        left_factor,
        r0,
        r1,
        r2,
        r3,
        r4,
        name="finish",
    )
    return (output, grad_tokens, grad_butterfly, grad_left, grad_right)


def solution(mesh):
    in_specs = (P("dp", "feat"), P("feat", None), P("feat", None), P(None, "feat"), P("dp", "feat"))
    out_specs = (
        P("dp", "feat"),
        P("dp", "feat"),
        P("feat", None),
        P("feat", None),
        P(None, "feat"),
    )
    return jax.shard_map(shards, mesh=mesh, in_specs=in_specs, out_specs=out_specs, check_vma=False)
```

```python
import functools

import jax
import jax.numpy as jnp
from jax import lax
from jax.experimental import pallas as pl
from jax.experimental.pallas import tpu as pltpu
from jax.sharding import Mesh
from jax.sharding import PartitionSpec as P

BF = jnp.bfloat16
F32 = jnp.float32
TILE = 256
PLANE = ("y", "z")
SMEM = pl.BlockSpec(memory_space=pltpu.SMEM)
ANY = pl.BlockSpec(memory_space=pl.ANY)
WHOLE = pl.BlockSpec()


def flip(block, axis, mask):
    count = lax.axis_size(axis)
    return lax.ppermute(block, axis, [(i, i ^ mask) for i in range(count)])


def normal_cdf(value):
    return 0.5 * (1.0 + lax.erf(value * 0.7071067811865476))


def contract(first, second, first_dim, second_dim):
    return lax.dot_general(
        first, second, (((first_dim,), (second_dim,)), ((), ())), preferred_element_type=F32
    )


def struct(*shape_and_type):
    *shape, kind = shape_and_type
    return jax.ShapeDtypeStruct(tuple(shape), kind)


def call(kernel, outs, *args, name, vmem=24, after=(), specs=None, gflop=0.0, **more):
    specs = list(specs) if specs else [WHOLE] * len(args)

    def body(*refs):
        kernel(*refs[: len(args)], *refs[len(args) + len(after) :])

    return pl.pallas_call(
        body,
        out_shape=outs,
        name=name,
        in_specs=specs + [ANY] * len(after),
        compiler_params=pltpu.CompilerParams(vmem_limit_bytes=vmem << 20),
        cost_estimate=pl.CostEstimate(flops=1000 + int(gflop * 1e9), bytes_accessed=1000, transcendentals=0),
        **more,
    )(*args, *after)


def low_kernel(x, w, o):
    o[...] = jnp.dot(x[...], w[...], preferred_element_type=F32).astype(BF)


def halves_kernel(x, a, b):
    rows = a.shape[0]
    a[...] = x[:rows, :]
    b[...] = x[rows:, :]


def copy_kernel(*refs):
    count = len(refs) // 2
    for x, o in zip(refs[:count], refs[count:]):
        o[...] = x[...]


def hold(arrays, after, name):
    return call(copy_kernel, [struct(*a.shape, a.dtype) for a in arrays], *arrays, name=name, after=after)


def sum_kernel(pieces, total):
    acc = pieces[0].astype(F32)
    for k in range(1, pieces.shape[0]):
        acc = acc + pieces[k].astype(F32)
    total[...] = acc


def spread_kernel(mine, other, copies):
    total = (mine[...] + other[...]).astype(BF)
    for k in range(copies.shape[0]):
        copies[k] = total


def gather_rows(mine, name, after=()):
    count = lax.axis_size(PLANE)
    other = flip(mine, "xl", 1)
    copies = call(
        spread_kernel, struct(count, *mine.shape, BF), mine, other, name=name, after=after
    )
    return copies, lax.all_to_all(copies, PLANE, 0, 0).reshape(-1, mine.shape[1])


def scatter_rows(part):
    count = lax.axis_size(PLANE)
    return lax.all_to_all(part.reshape(count, -1, part.shape[1]), PLANE, 0, 0)


def row_sum(pieces, name, after=()):
    return call(sum_kernel, struct(*pieces.shape[1:], F32), pieces, name=name, after=after)


def forward_kernel(start, whole, reduced, right, cotangent, weight, *refs):
    blocks, (output, delta) = refs[:-2], refs[-2:]
    rows, bs = delta.shape
    for row in range(0, rows, TILE):
        here = slice(row, row + TILE)
        there = slice(start + row, start + row + TILE)
        pre = jnp.dot(reduced[there, :], right[...], preferred_element_type=F32)
        for slot, ref in enumerate(blocks):
            pre = pre + jnp.dot(
                ref[there if whole[slot] else here, :],
                weight[:, slot * bs : (slot + 1) * bs],
                preferred_element_type=F32,
            )
        cdf = normal_cdf(pre)
        output[here, :] = (pre * cdf).astype(BF)
        density = jnp.exp(-0.5 * pre * pre) * 0.3989422804014327
        delta[here, :] = (cotangent[there, :].astype(F32) * (cdf + pre * density)).astype(BF)


def slot_dots(slots, blocks, cols):
    out = []
    for parts in slots:
        total = None
        if len(parts) == len(cols):
            pairs = [(blocks[k][...], col) for k, col in zip(parts, cols)]
        else:
            step = cols[0].shape[0]
            pairs = [
                (blocks[parts[0]][n * step : (n + 1) * step, :], col) for n, col in enumerate(cols)
            ]
        for block, col in pairs:
            term = contract(block, col, 0, 0)
            total = term if total is None else total + term
        out.append(total)
    return out


def give_kernel(slots, n, core, *refs):
    deltas, blocks, out = refs[:n], refs[n:-1], refs[-1]
    hc = out.shape[1]

    def run(first):
        row = 0
        cols = [d[:, first : first + hc] for d in deltas]
        for total in slot_dots(sum(slots, ()), blocks, cols):
            out[row : row + total.shape[0], :] = total.astype(out.dtype)
            row += total.shape[0]

    pl.when(core[0] == 0)(lambda: run(hc))
    pl.when(core[0] == 1)(lambda: run(0))


def keep_kernel(slots, n, core, got, *refs):
    deltas, blocks, outs = refs[:n], refs[n : -len(slots)], refs[-len(slots) :]
    hc = got.shape[1]

    def run(first):
        start = 0
        cols = [d[:, first : first + hc] for d in deltas]
        for group, out in zip(slots, outs):
            row = 0
            for total in slot_dots(group, blocks, cols):
                size = total.shape[0]
                other = got[start : start + size, :].astype(F32)
                out[row : row + size, :] = (total + other).astype(out.dtype)
                row += size
                start += size

    pl.when(core[0] == 0)(lambda: run(0))
    pl.when(core[0] == 1)(lambda: run(hc))


def local_back_kernel(delta_a, delta_b, right, low):
    half = delta_a.shape[0]
    for first, delta in ((0, delta_a), (half, delta_b)):
        low[first : first + half, :] = contract(delta[...], right[...], 1, 1).astype(BF)


def back_kernel(slots, delta_a, delta_b, weight, *outs):
    half, bs = delta_a.shape
    for slot, out in zip(slots, outs):
        for first, delta in ((0, delta_a), (half, delta_b)):
            out[first : first + half, :] = contract(
                delta[...], weight[:, slot * bs : (slot + 1) * bs], 1, 1
            ).astype(BF)


def back_add_kernel(slot, delta_a, delta_b, weight, got, out):
    half, bs = delta_a.shape
    for first, delta in ((0, delta_a), (half, delta_b)):
        here = slice(first, first + half)
        term = contract(delta[...], weight[:, slot * bs : (slot + 1) * bs], 1, 1)
        out[here, :] = (term + got[here, :].astype(F32)).astype(BF)


def finish_kernel(delta_a, delta_b, weight, back_reduced, left, *refs):
    parts, out = refs[:-1], refs[-1]
    half, bs = delta_a.shape
    for first, delta in ((0, delta_a), (half, delta_b)):
        for row in range(0, half, TILE):
            here = slice(first + row, first + row + TILE)
            total = contract(delta[row : row + TILE, :], weight[:, :bs], 1, 1)
            total = total + contract(back_reduced[here, :], left[...], 1, 1)
            for part in parts:
                total = total + part[here, :].astype(F32)
            out[here, :] = total.astype(BF)


def assemble_kernel(with_old, core, *refs):
    mine, recv, mine_o, recv_o = refs[:4]
    out = refs[4 + with_old]

    def run(a, b, c, d):
        hc = a.shape[1]
        out[:, :hc] = a[...].astype(F32) + b[...].astype(F32)
        out[:, hc:] = c[...].astype(F32) + d[...].astype(F32)

    pl.when(core[0] == 0)(lambda: run(mine, recv, mine_o, recv_o))
    pl.when(core[0] == 1)(lambda: run(mine_o, recv_o, mine, recv))


def assemble(core, four, out, steps, in_start, out_start, old, name):
    hc = four[0].shape[1]
    bs = out.shape[0]
    half = pl.BlockSpec((bs, hc), lambda k: (k + in_start, 0))
    more = {}
    specs = [SMEM] + [half] * 4
    args = [core, *four]
    if old is not None:
        specs.append(pl.BlockSpec(memory_space=pl.ANY))
        args.append(old)
        more["input_output_aliases"] = {5: 0}
    return call(
        functools.partial(assemble_kernel, old is not None),
        out,
        *args,
        name=name,
        grid=(steps,),
        specs=specs,
        out_specs=pl.BlockSpec((bs, 2 * hc), lambda k: (0, k + out_start)),
        **more,
    )


def pick(slots, blocks):
    used = [k for group in slots for parts in group for k in parts]
    local = tuple(tuple(tuple(used.index(k) for k in parts) for parts in group) for group in slots)
    heights = [sum(blocks[parts[0]].shape[1] for parts in group) for group in slots]
    return local, [blocks[k] for k in used], heights


def give_half(core, slots, deltas, blocks, name, after=(), gflop=0.0):
    local, used, heights = pick(slots, blocks)
    n = len(deltas)
    give = call(
        functools.partial(give_kernel, local, n),
        [struct(sum(heights), deltas[0].shape[1] // 2, BF)],
        core,
        *deltas,
        *used,
        name="give_" + name,
        specs=[SMEM] + [WHOLE] * (n + len(used)),
        after=after,
        gflop=gflop,
    )
    return flip(give[0], "core", 1)


def keep_half(core, got, slots, deltas, blocks, name, after=(), gflop=0.0):
    local, used, heights = pick(slots, blocks)
    n = len(deltas)
    return call(
        functools.partial(keep_kernel, local, n),
        [struct(height, got.shape[1], BF) for height in heights],
        core,
        got,
        *deltas,
        *used,
        name="keep_" + name,
        specs=[SMEM] + [WHOLE] * (1 + n + len(used)),
        after=after,
        gflop=gflop,
    )


def over_chips(mine):
    recv = flip(mine, "xh", 1)
    return mine, recv, flip(mine, "core", 1), flip(recv, "core", 1)


def shards(tokens, butterfly, left_factor, right_factor, cotangent):
    rows, bs = tokens.shape
    rank = left_factor.shape[1]
    half = rows // 2
    core = lax.axis_index("core").astype(jnp.int32).reshape(1)

    t0 = flip(tokens, "xl", 1)
    first, second = call(halves_kernel, (struct(half, bs, BF),) * 2, tokens, name="halves")
    t1a, t3a = flip(first, "z", 1), flip(first, "y", 1)
    low = call(low_kernel, struct(rows, rank, BF), tokens, left_factor, name="low")
    low_mine = row_sum(scatter_rows(low), "low_sum", (t0, t1a, t3a))
    t1b, t3b = flip(second, "z", 1), flip(second, "y", 1)
    t2a, t4a = flip(t1a, "z", 3), flip(t3a, "y", 3)
    copies, reduced = gather_rows(low_mine, "low_spread")
    held = hold((t1b, t3b), (copies,), "hold_b")
    t2b, t4b = flip(held[0], "z", 3), flip(held[1], "y", 3)

    whole = (True, True, False, False, False, False)
    outs, deltas = [], []
    for start, parts, name in (
        (0, (t1a, t2a, t3a, t4a), "forward_a"),
        (half, (t1b, t2b, t3b, t4b), "forward_b"),
    ):
        out, delta = call(
            functools.partial(forward_kernel, start, whole),
            (struct(half, bs, BF), struct(half, bs, BF)),
            reduced,
            right_factor,
            cotangent,
            butterfly,
            tokens,
            t0,
            *parts,
            name=name,
            after=tuple(deltas),
            gflop=4.5,
        )
        outs.append(out)
        deltas.append(delta)
    output = jnp.concatenate(outs, axis=0)

    full = struct(rows, bs, BF)
    (c0,) = call(
        functools.partial(back_kernel, (1,)), (full,), *deltas, butterfly, name="back_x", gflop=1.0
    )
    r0 = flip(c0, "xl", 1)
    local_back = call(
        local_back_kernel,
        struct(rows, rank, BF),
        *deltas,
        right_factor,
        name="local_back",
        after=(c0,),
        gflop=0.5,
    )
    back_pieces = scatter_rows(local_back)
    blocks = (tokens, t0, t1a, t1b, t2a, t2b, t3a, t3b, t4a, t4b, reduced)
    slots = (((0,), (1,), (2, 3)), ((4, 5), (6, 7), (8, 9), (10,)))
    got = give_half(core, slots, deltas, blocks, "all", (local_back,), gflop=4.5)
    mine0, mine1 = keep_half(core, got, slots, deltas, blocks, "all", gflop=4.5)
    c2, c4 = call(
        functools.partial(back_kernel, (3, 5)),
        (full,) * 2,
        *deltas,
        butterfly,
        name="back_far",
        after=(back_pieces, mine0),
        gflop=2.0,
    )
    g2, g4 = flip(c2, "z", 3), flip(c4, "y", 3)
    back_mine = row_sum(back_pieces, "back_sum", (r0, c2))
    mine0, mine1 = hold((mine0, mine1), (back_mine,), "hold_halves")
    four0, four1 = over_chips(mine0), over_chips(mine1)
    copies, back_reduced = gather_rows(back_mine, "back_spread", (mine0, mine1))
    s1 = call(
        functools.partial(back_add_kernel, 2),
        full,
        *deltas,
        butterfly,
        g2,
        name="back_z",
        after=(copies,),
        gflop=2.0,
    )
    s3 = call(
        functools.partial(back_add_kernel, 4),
        full,
        *deltas,
        butterfly,
        g4,
        name="back_y",
        after=(copies,),
        gflop=2.0,
    )
    r1, r3 = flip(s1, "z", 1), flip(s3, "y", 1)
    left_slots = (((0,),),)
    left_got = give_half(core, left_slots, [back_reduced], blocks, "left", (s1, s3), gflop=0.5)
    (mine2,) = keep_half(core, left_got, left_slots, [back_reduced], blocks, "left", gflop=0.5)
    left_four = over_chips(mine2)

    grads = struct(*butterfly.shape, F32)
    grads_a = assemble(core, four0, grads, 3, 0, 0, None, "put0")
    grad_butterfly = assemble(core, four1, grads, 3, 0, 3, grads_a, "put1")
    grad_right = assemble(core, four1, struct(rank, bs, F32), 1, 3 * bs // rank, 0, None, "put_right")
    grad_left = assemble(core, left_four, struct(bs, rank, F32), 1, 0, 0, None, "put_left")

    grad_tokens = call(
        finish_kernel, full, *deltas, butterfly, back_reduced, left_factor, r0, r1, r3, name="finish"
    )
    return (output, grad_tokens, grad_butterfly, grad_left, grad_right)


def solution(mesh):
    axes = ("xh", "core", "y", "z", "xl")
    mesh = Mesh(mesh.devices.reshape(2, 2, 4, 4, 2), axes)
    dp, feat = axes[:2], axes[2:]
    in_specs = (P(dp, feat), P(feat, None), P(feat, None), P(None, feat), P(dp, feat))
    out_specs = (P(dp, feat), P(dp, feat), P(feat, None), P(feat, None), P(None, feat))
    return jax.shard_map(shards, mesh=mesh, in_specs=in_specs, out_specs=out_specs, check_vma=False)
```

```python
import functools

import jax
import jax.numpy as jnp
from jax import lax
from jax.experimental import pallas as pl
from jax.experimental.pallas import tpu as pltpu
from jax.sharding import Mesh
from jax.sharding import PartitionSpec as P

BF = jnp.bfloat16
F32 = jnp.float32
TILE = 256
PLANE = ("y", "z")
SMEM = pl.BlockSpec(memory_space=pltpu.SMEM)
ANY = pl.BlockSpec(memory_space=pl.ANY)
WHOLE = pl.BlockSpec()


def flip(block, axis, mask):
    count = lax.axis_size(axis)
    return lax.ppermute(block, axis, [(i, i ^ mask) for i in range(count)])


def normal_cdf(value):
    return 0.5 * (1.0 + lax.erf(value * 0.7071067811865476))


def contract(first, second, first_dim, second_dim):
    return lax.dot_general(
        first, second, (((first_dim,), (second_dim,)), ((), ())), preferred_element_type=F32
    )


def struct(*shape_and_type):
    *shape, kind = shape_and_type
    return jax.ShapeDtypeStruct(tuple(shape), kind)


def call(kernel, outs, *args, name, vmem=24, after=(), specs=None, gflop=0.0, **more):
    specs = list(specs) if specs else [WHOLE] * len(args)

    def body(*refs):
        kernel(*refs[: len(args)], *refs[len(args) + len(after) :])

    return pl.pallas_call(
        body,
        out_shape=outs,
        name=name,
        in_specs=specs + [ANY] * len(after),
        compiler_params=pltpu.CompilerParams(vmem_limit_bytes=vmem << 20),
        cost_estimate=pl.CostEstimate(flops=1000 + int(gflop * 1e9), bytes_accessed=1000, transcendentals=0),
        **more,
    )(*args, *after)


def low_kernel(x, w, o):
    o[...] = jnp.dot(x[...], w[...], preferred_element_type=F32).astype(BF)


def halves_kernel(x, a, b):
    rows = a.shape[0]
    a[...] = x[:rows, :]
    b[...] = x[rows:, :]


def copy_kernel(*refs):
    count = len(refs) // 2
    for x, o in zip(refs[:count], refs[count:]):
        o[...] = x[...]


def hold(arrays, after, name):
    return call(copy_kernel, [struct(*a.shape, a.dtype) for a in arrays], *arrays, name=name, after=after)


def sum_kernel(pieces, total):
    acc = pieces[0].astype(F32)
    for k in range(1, pieces.shape[0]):
        acc = acc + pieces[k].astype(F32)
    total[...] = acc


def spread_kernel(mine, other, copies):
    total = (mine[...] + other[...]).astype(BF)
    for k in range(copies.shape[0]):
        copies[k] = total


def gather_rows(mine, other, name, after=()):
    count = lax.axis_size(PLANE)
    copies = call(
        spread_kernel, struct(count, *mine.shape, BF), mine, other, name=name, after=after
    )
    return copies, lax.all_to_all(copies, PLANE, 0, 0).reshape(-1, mine.shape[1])


def scatter_rows(part):
    count = lax.axis_size(PLANE)
    return lax.all_to_all(part.reshape(count, -1, part.shape[1]), PLANE, 0, 0)


def row_sum(pieces, name, after=()):
    return call(sum_kernel, struct(*pieces.shape[1:], F32), pieces, name=name, after=after)


def forward_kernel(start, whole, reduced, right, cotangent, weight, *refs):
    blocks, (output, delta) = refs[:-2], refs[-2:]
    rows, bs = delta.shape
    for row in range(0, rows, TILE):
        here = slice(row, row + TILE)
        there = slice(start + row, start + row + TILE)
        pre = jnp.dot(reduced[there, :], right[...], preferred_element_type=F32)
        for slot, ref in enumerate(blocks):
            pre = pre + jnp.dot(
                ref[there if whole[slot] else here, :],
                weight[:, slot * bs : (slot + 1) * bs],
                preferred_element_type=F32,
            )
        cdf = normal_cdf(pre)
        output[here, :] = (pre * cdf).astype(BF)
        density = jnp.exp(-0.5 * pre * pre) * 0.3989422804014327
        delta[here, :] = (cotangent[there, :].astype(F32) * (cdf + pre * density)).astype(BF)


def slot_dots(slots, blocks, cols):
    out = []
    for parts in slots:
        total = None
        if len(parts) == len(cols):
            pairs = [(blocks[k][...], col) for k, col in zip(parts, cols)]
        else:
            step = cols[0].shape[0]
            pairs = [
                (blocks[parts[0]][n * step : (n + 1) * step, :], col) for n, col in enumerate(cols)
            ]
        for block, col in pairs:
            term = contract(block, col, 0, 0)
            total = term if total is None else total + term
        out.append(total)
    return out


def give_kernel(slots, n, core, *refs):
    deltas, blocks, out = refs[:n], refs[n:-1], refs[-1]
    hc = out.shape[1]

    def run(first):
        row = 0
        cols = [d[:, first : first + hc] for d in deltas]
        for total in slot_dots(sum(slots, ()), blocks, cols):
            out[row : row + total.shape[0], :] = total.astype(out.dtype)
            row += total.shape[0]

    pl.when(core[0] == 0)(lambda: run(hc))
    pl.when(core[0] == 1)(lambda: run(0))


def keep_kernel(slots, n, core, got, *refs):
    deltas, blocks, outs = refs[:n], refs[n : -len(slots)], refs[-len(slots) :]
    hc = got.shape[1]

    def run(first):
        start = 0
        cols = [d[:, first : first + hc] for d in deltas]
        for group, out in zip(slots, outs):
            row = 0
            for total in slot_dots(group, blocks, cols):
                size = total.shape[0]
                other = got[start : start + size, :].astype(F32)
                out[row : row + size, :] = (total + other).astype(out.dtype)
                row += size
                start += size

    pl.when(core[0] == 0)(lambda: run(0))
    pl.when(core[0] == 1)(lambda: run(hc))


def local_back_kernel(delta_a, delta_b, right, low):
    half = delta_a.shape[0]
    for first, delta in ((0, delta_a), (half, delta_b)):
        low[first : first + half, :] = contract(delta[...], right[...], 1, 1).astype(BF)


def back_kernel(slots, delta_a, delta_b, weight, *outs):
    half, bs = delta_a.shape
    for slot, out in zip(slots, outs):
        for first, delta in ((0, delta_a), (half, delta_b)):
            out[first : first + half, :] = contract(
                delta[...], weight[:, slot * bs : (slot + 1) * bs], 1, 1
            ).astype(BF)


def back_add_kernel(slot, delta_a, delta_b, weight, got, out):
    half, bs = delta_a.shape
    for first, delta in ((0, delta_a), (half, delta_b)):
        here = slice(first, first + half)
        term = contract(delta[...], weight[:, slot * bs : (slot + 1) * bs], 1, 1)
        out[here, :] = (term + got[here, :].astype(F32)).astype(BF)


def finish_kernel(delta_a, delta_b, weight, back_reduced, left, *refs):
    parts, out = refs[:-1], refs[-1]
    half, bs = delta_a.shape
    for first, delta in ((0, delta_a), (half, delta_b)):
        for row in range(0, half, TILE):
            here = slice(first + row, first + row + TILE)
            total = contract(delta[row : row + TILE, :], weight[:, :bs], 1, 1)
            total = total + contract(back_reduced[here, :], left[...], 1, 1)
            for part in parts:
                total = total + part[here, :].astype(F32)
            out[here, :] = total.astype(BF)


def add_kernel(mine, recv, total):
    total[...] = mine[...].astype(F32) + recv[...].astype(F32)


def assemble_kernel(with_old, core, *refs):
    mine, other = refs[:2]
    out = refs[2 + with_old]
    hc = mine.shape[1]

    def run(a, b):
        out[:, :hc] = a[...]
        out[:, hc:] = b[...]

    pl.when(core[0] == 0)(lambda: run(mine, other))
    pl.when(core[0] == 1)(lambda: run(other, mine))


def assemble(core, two, out, steps, in_start, out_start, old, name):
    hc = two[0].shape[1]
    bs = out.shape[0]
    half = pl.BlockSpec((bs, hc), lambda k: (k + in_start, 0))
    more = {}
    specs = [SMEM] + [half] * 2
    args = [core, *two]
    if old is not None:
        specs.append(pl.BlockSpec(memory_space=pl.ANY))
        args.append(old)
        more["input_output_aliases"] = {3: 0}
    return call(
        functools.partial(assemble_kernel, old is not None),
        out,
        *args,
        name=name,
        grid=(steps,),
        specs=specs,
        out_specs=pl.BlockSpec((bs, 2 * hc), lambda k: (0, k + out_start)),
        **more,
    )


def pick(slots, blocks):
    used = [k for group in slots for parts in group for k in parts]
    local = tuple(tuple(tuple(used.index(k) for k in parts) for parts in group) for group in slots)
    heights = [sum(blocks[parts[0]].shape[1] for parts in group) for group in slots]
    return local, [blocks[k] for k in used], heights


def give_half(core, slots, deltas, blocks, name, after=(), gflop=0.0):
    local, used, heights = pick(slots, blocks)
    n = len(deltas)
    give = call(
        functools.partial(give_kernel, local, n),
        [struct(sum(heights), deltas[0].shape[1] // 2, BF)],
        core,
        *deltas,
        *used,
        name="give_" + name,
        specs=[SMEM] + [WHOLE] * (n + len(used)),
        after=after,
        gflop=gflop,
    )
    return flip(give[0], "core", 1)


def keep_half(core, got, slots, deltas, blocks, name, after=(), gflop=0.0):
    local, used, heights = pick(slots, blocks)
    n = len(deltas)
    return call(
        functools.partial(keep_kernel, local, n),
        [struct(height, got.shape[1], BF) for height in heights],
        core,
        got,
        *deltas,
        *used,
        name="keep_" + name,
        specs=[SMEM] + [WHOLE] * (1 + n + len(used)),
        after=after,
        gflop=gflop,
    )


def over_chips(mine, name, after=()):
    total = call(add_kernel, struct(*mine.shape, F32), mine, flip(mine, "xh", 1), name="add_" + name, after=after)
    return total, flip(total, "core", 1)


def shards(tokens, butterfly, left_factor, right_factor, cotangent):
    rows, bs = tokens.shape
    rank = left_factor.shape[1]
    half = rows // 2
    core = lax.axis_index("core").astype(jnp.int32).reshape(1)

    t0 = flip(tokens, "xl", 1)
    first, second = call(halves_kernel, (struct(half, bs, BF),) * 2, tokens, name="halves")
    t1a, t3a = flip(first, "z", 1), flip(first, "y", 1)
    low = call(low_kernel, struct(rows, rank, BF), tokens, left_factor, name="low")
    low_mine = row_sum(scatter_rows(low), "low_sum", (t0, t1a, t3a))
    t1b, t3b = flip(second, "z", 1), flip(second, "y", 1)
    t2a, t4a = flip(t1a, "z", 3), flip(t3a, "y", 3)
    copies, reduced = gather_rows(low_mine, flip(low_mine, "xl", 1), "low_spread")
    held = hold((t1b, t3b), (copies,), "hold_b")
    t2b, t4b = flip(held[0], "z", 3), flip(held[1], "y", 3)

    whole = (True, True, False, False, False, False)
    outs, deltas = [], []
    for start, parts, name in (
        (0, (t1a, t2a, t3a, t4a), "forward_a"),
        (half, (t1b, t2b, t3b, t4b), "forward_b"),
    ):
        out, delta = call(
            functools.partial(forward_kernel, start, whole),
            (struct(half, bs, BF), struct(half, bs, BF)),
            reduced,
            right_factor,
            cotangent,
            butterfly,
            tokens,
            t0,
            *parts,
            name=name,
            after=tuple(deltas),
            gflop=4.5,
        )
        outs.append(out)
        deltas.append(delta)
    output = jnp.concatenate(outs, axis=0)

    full = struct(rows, bs, BF)
    (c0,) = call(
        functools.partial(back_kernel, (1,)), (full,), *deltas, butterfly, name="back_x", gflop=1.0
    )
    r0 = flip(c0, "xl", 1)
    local_back = call(
        local_back_kernel,
        struct(rows, rank, BF),
        *deltas,
        right_factor,
        name="local_back",
        after=(c0,),
        gflop=0.5,
    )
    back_pieces = scatter_rows(local_back)
    blocks = (tokens, t0, t1a, t1b, t2a, t2b, t3a, t3b, t4a, t4b, reduced)
    slots = (((0,), (1,), (2, 3)), ((4, 5), (6, 7), (8, 9), (10,)))
    got = give_half(core, slots, deltas, blocks, "all", (local_back,), gflop=4.5)
    mine0, mine1 = keep_half(core, got, slots, deltas, blocks, "all", gflop=4.5)
    c2, c4 = call(
        functools.partial(back_kernel, (3, 5)),
        (full,) * 2,
        *deltas,
        butterfly,
        name="back_far",
        after=(back_pieces, mine0),
        gflop=2.0,
    )
    g2, g4 = flip(c2, "z", 3), flip(c4, "y", 3)
    back_mine = row_sum(back_pieces, "back_sum", (r0, c2))
    back_other = flip(back_mine, "xl", 1)
    mine0, mine1 = hold((mine0, mine1), (back_other,), "hold_halves")
    copies, back_reduced = gather_rows(back_mine, back_other, "back_spread", (mine0, mine1))
    s1 = call(
        functools.partial(back_add_kernel, 2),
        full,
        *deltas,
        butterfly,
        g2,
        name="back_z",
        after=(copies,),
        gflop=2.0,
    )
    s3 = call(
        functools.partial(back_add_kernel, 4),
        full,
        *deltas,
        butterfly,
        g4,
        name="back_y",
        after=(copies,),
        gflop=2.0,
    )
    r1, r3 = flip(s1, "z", 1), flip(s3, "y", 1)
    left_slots = (((0,),),)
    left_got = give_half(core, left_slots, [back_reduced], blocks, "left", (s1, s3), gflop=0.5)
    (mine2,) = keep_half(core, left_got, left_slots, [back_reduced], blocks, "left", gflop=0.5)
    left_four = over_chips(mine2, "left")
    four0, four1 = over_chips(mine0, "0", (mine2,)), over_chips(mine1, "1", (mine2,))

    grads = struct(*butterfly.shape, F32)
    grads_a = assemble(core, four0, grads, 3, 0, 0, None, "put0")
    grad_butterfly = assemble(core, four1, grads, 3, 0, 3, grads_a, "put1")
    grad_right = assemble(core, four1, struct(rank, bs, F32), 1, 3 * bs // rank, 0, None, "put_right")
    grad_left = assemble(core, left_four, struct(bs, rank, F32), 1, 0, 0, None, "put_left")

    grad_tokens = call(
        finish_kernel, full, *deltas, butterfly, back_reduced, left_factor, r0, r1, r3, name="finish", gflop=15.0
    )
    return (output, grad_tokens, grad_butterfly, grad_left, grad_right)


def solution(mesh):
    axes = ("xh", "core", "y", "z", "xl")
    mesh = Mesh(mesh.devices.reshape(2, 2, 4, 4, 2), axes)
    dp, feat = axes[:2], axes[2:]
    in_specs = (P(dp, feat), P(feat, None), P(feat, None), P(None, feat), P(dp, feat))
    out_specs = (P(dp, feat), P(dp, feat), P(feat, None), P(feat, None), P(None, feat))
    return jax.shard_map(shards, mesh=mesh, in_specs=in_specs, out_specs=out_specs, check_vma=False)
```
